32 devices in a mesh: sky: 8 (over z, x), src: 4 (over y, core).
Axes of the slice: x: 2, y: 2, z: 4, core: 2. Of those that a mesh axis runs over, the one named last changes fastest.
Arguments:
- exposures: float32 [8, 64, 256, 256], P('sky', 'src'), may hold values from -6 to 6
- variance: float32 [8, 64, 256, 256], P('sky', 'src'), may hold values from 0.25 to 4
- coef_table: float32 [64, 45], replicated, may hold values from -6 to 6
- coef_index: int32 [8, 64], P('sky', 'src'), may hold values from 0 to 63
- offsets: int32 [8, 64, 2], P('sky', 'src'), may hold values from 0 to 256
- tile_codes: int32 [8, 64], P('sky', 'src'), may hold values from 0 to 7, as said below
- detect_ra: float32 [41], replicated, may hold values from -1 to 1
- detect_dec: float32 [41], replicated, may hold values from -1 to 1
Outputs:
- coadd: float32 [4096, 2048], P('sky', 'src')
- detection: float32 [4096, 2048], P('sky', 'src')
The draws below stay inside these ranges and needn't reach their ends.
Inputs may be any that keep to these rules, and one draw needn't show every extreme that they name: `tile_codes`: code c sends a tile to the patch row c // 4 after the holder's own (wrapping around) and to owner c mod 4 along src. On one device at most 2 tiles name the same code; in every sky row one code is named by exactly 2 tiles on every device of that row.
All inputs are finite; a program needn't handle non-finite values.
Results may differ from the reference program's by a relative error of at most 0.0003.
Values sent between devices are 32-bit elements; how exact they have to be, the bound alone decides.
A program may use at most 192 MiB of HBM per device.

```python
import math
import jax
import jax.numpy as jnp
from jax import lax

TILE = 256
PATCH = 512
TILES_DEV = 16
NBASIS = 45
KSIZE = 21
DSIZE = 41
RIM = 20
NCOEF = 64
OWNERS = 4
RA_PATCHES = 8


def draw_tile_codes(key, part):
    code_total = 2 * OWNERS
    key_hot, key_order, key_place = jax.random.split(key, 3)
    hottest = jax.random.randint(key_hot, (RA_PATCHES,), 0, code_total)
    entries = jnp.arange(2 * code_total, dtype=jnp.int32)
    raw_scores = jax.random.randint(key_order, (RA_PATCHES, OWNERS, 2 * code_total), 0, 1048576)
    scores = raw_scores * (2 * code_total) + entries[None, None, :]
    is_hot = (entries % code_total)[None, None, :] == hottest[:, None, None]
    scores = jnp.where(is_hot, entries[None, None, :] - 2 * code_total, scores)
    ordering = jnp.argsort(scores, axis=-1, stable=True)
    chosen = (ordering[..., :TILES_DEV] % code_total).astype(jnp.int32)
    place_scores = jax.random.randint(key_place, (RA_PATCHES, OWNERS, TILES_DEV), 0, 1048576) * TILES_DEV + jnp.arange(TILES_DEV, dtype=jnp.int32)[None, None, :]
    shuffle = jnp.argsort(place_scores, axis=-1, stable=True)
    chosen = jnp.take_along_axis(chosen, shuffle, axis=-1)
    return chosen.reshape(RA_PATCHES, OWNERS * TILES_DEV).astype(jnp.int32)


def place_ends(result, key, smallest, largest):
    longest = result.shape.index(max(result.shape))
    spots = []
    for shift in (0, 1):
        where = [jax.random.randint(jax.random.fold_in(key, axis), (), 0, length) for axis, length in enumerate(result.shape)]
        where[longest] = (where[longest] + shift) % result.shape[longest]
        spots.append(tuple(where))
    return result.at[spots[0]].set(smallest).at[spots[1]].set(largest)


def block_levels(own_key, shape, cuts, least, top_value):
    level = 1.0
    for dim, parts in cuts:
        steps = jax.random.uniform(jax.random.fold_in(jax.random.fold_in(own_key, 6), dim), (parts,), jnp.float32, least / len(cuts), top_value / len(cuts))
        level = level * jnp.repeat(jnp.exp(steps), shape[dim] // parts).reshape((-1,) + (1,) * (len(shape) - 1 - dim))
    return level


def scatter_about(own_key, shape, deviation, bound, shards=(), held_as=jnp.bfloat16):
    drawn = deviation * jax.random.normal(own_key, shape, jnp.float32)
    if shards:
        drawn = drawn * block_levels(own_key, shape, shards, -0.22, 0.18)
    return jnp.clip(drawn, -bound, bound).astype(held_as)


def setup_inputs(seed: int = 0) -> dict:
    key_of = jax.random.split(jax.random.key(seed), 9)
    return {
        "exposures": scatter_about(key_of[0], (RA_PATCHES, OWNERS * TILES_DEV, TILE, TILE), 1.0, 6.0, ((0, 8), (1, 4)), jnp.float32),
        "variance": jnp.clip(jnp.exp(math.log(4.0) - 2.7725887 * jax.random.uniform(key_of[1], (RA_PATCHES, OWNERS * TILES_DEV, TILE, TILE), jnp.float32) ** block_levels(key_of[1], (RA_PATCHES, OWNERS * TILES_DEV, TILE, TILE), ((0, 8), (1, 4)), -0.2, 0.2)), 0.25, 4.0),
        "coef_table": scatter_about(key_of[2], (NCOEF, NBASIS), 1.0, 6.0, (), jnp.float32),
        "coef_index": place_ends(jax.random.randint(key_of[3], (RA_PATCHES, OWNERS * TILES_DEV), 0, NCOEF), jax.random.fold_in(key_of[3], 1), 0, NCOEF - 1).astype(jnp.int32),
        "offsets": place_ends(jax.random.randint(key_of[4], (RA_PATCHES, OWNERS * TILES_DEV, 2), 0, PATCH - TILE + 1), jax.random.fold_in(key_of[4], 1), 0, PATCH - TILE).astype(jnp.int32),
        "tile_codes": draw_tile_codes(jax.random.fold_in(key_of[8], 71), 0),
        "detect_ra": scatter_about(key_of[6], (DSIZE,), DSIZE ** -0.5, 1.0, (), jnp.float32),
        "detect_dec": scatter_about(key_of[7], (DSIZE,), DSIZE ** -0.5, 1.0, (), jnp.float32),
    }


SPREADS = (0.75, 1.5, 3.0)


def basis_filters():
    radius = KSIZE // 2
    centred = jnp.arange(KSIZE, dtype=jnp.float32) - radius
    along_x = []
    along_y = []
    for spread in SPREADS:
        gaussian = jnp.exp(-(centred * centred) / (2.0 * spread * spread))
        scaled = centred / spread
        for power_x in range(5):
            for power_y in range(5 - power_x):
                filter_x = gaussian * scaled ** power_x
                filter_y = gaussian * scaled ** power_y
                along_x.append(filter_x / jnp.sum(jnp.abs(filter_x)))
                along_y.append(filter_y / jnp.sum(jnp.abs(filter_y)))
    return jnp.stack(along_y, 1), jnp.stack(along_x, 1)


def psf_kernel(coefs, along_y, along_x):
    return jnp.dot(along_y * coefs[None, :], along_x.T, precision=lax.Precision.HIGHEST, preferred_element_type=jnp.float32)


def match_fft(exposure, kernel):
    radius = KSIZE // 2
    extent = exposure.shape[0]
    full_len = extent + 2 * radius
    flipped = kernel[::-1, ::-1]
    spectrum = jnp.fft.rfft2(exposure, s=(full_len, full_len)) * jnp.fft.rfft2(flipped, s=(full_len, full_len))
    whole = jnp.fft.irfft2(spectrum, s=(full_len, full_len))
    return whole[radius:radius + extent, radius:radius + extent].astype(jnp.float32)


def reference(exposures, variance, coef_table, coef_index, offsets, tile_codes, detect_ra, detect_dec):
    along_y, along_x = basis_filters()
    per_row = exposures.shape[1]
    flat_tiles = exposures.reshape(-1, TILE, TILE)
    flat_var = variance.reshape(-1, TILE, TILE)
    flat_index = coef_index.reshape(-1).astype(jnp.int32)
    flat_offsets = offsets.reshape(-1, 2).astype(jnp.int32)
    flat_codes = tile_codes.reshape(-1).astype(jnp.int32)
    sky_rows = (jnp.arange(flat_codes.shape[0]) // per_row).astype(jnp.int32)

    def weighted_match(entry):
        exposure, var_tile, index_one = entry
        kernel = psf_kernel(coef_table[index_one], along_y, along_x)
        weight_map = 1.0 / var_tile
        return weight_map * match_fft(exposure, kernel), weight_map

    matched, weights = lax.map(weighted_match, (flat_tiles, flat_var, flat_index))

    def accumulate(totals, entry):
        numerator, denominator = totals
        matched_one, weight_one, corner, code_one, row_one = entry
        dest_row = ((row_one + code_one // OWNERS) % RA_PATCHES) * PATCH + corner[0]
        dest_col = (code_one % OWNERS) * PATCH + corner[1]
        anchor = (dest_row.astype(jnp.int32), dest_col.astype(jnp.int32))
        numerator = lax.dynamic_update_slice(numerator, lax.dynamic_slice(numerator, anchor, (TILE, TILE)) + matched_one, anchor)
        denominator = lax.dynamic_update_slice(denominator, lax.dynamic_slice(denominator, anchor, (TILE, TILE)) + weight_one, anchor)
        return (numerator, denominator), None

    blank = jnp.zeros((RA_PATCHES * PATCH, OWNERS * PATCH), jnp.float32)
    totals, ignored = lax.scan(accumulate, (blank, blank), (matched, weights, flat_offsets, flat_codes, sky_rows))
    numerator, denominator = totals
    coadd = numerator / (denominator + 1.0)
    grid_rows = coadd.shape[0]
    grid_cols = coadd.shape[1]
    col_padded = jnp.pad(coadd, ((0, 0), (RIM, RIM)))
    filtered = jnp.zeros_like(coadd)
    for tap_index in range(DSIZE):
        filtered = filtered + detect_dec[tap_index] * col_padded[:, tap_index:tap_index + grid_cols]
    wrapped = jnp.concatenate([filtered[grid_rows - RIM:], filtered, filtered[:RIM]], 0)
    detection = jnp.zeros_like(coadd)
    for tap_index in range(DSIZE):
        detection = detection + detect_ra[tap_index] * wrapped[tap_index:tap_index + grid_rows]
    return coadd, detection
```

```python
import functools

import numpy as np
import jax
import jax.numpy as jnp
from jax import lax
from jax.experimental import pallas as pl
from jax.experimental.pallas import tpu as pltpu
from jax.sharding import PartitionSpec as P

CAP = 2
KSIZE = 21
SPREADS = (0.75, 1.5, 3.0)
LANES = 128
LEAD = 16
ROWS = 64
HIGHEST = lax.Precision.HIGHEST


def basis_filters():
    centred = np.arange(KSIZE, dtype=np.float64) - KSIZE // 2
    along_x, along_y = [], []
    for spread in SPREADS:
        gaussian = np.exp(-(centred * centred) / (2.0 * spread * spread))
        scaled = centred / spread
        for power_x in range(5):
            for power_y in range(5 - power_x):
                filter_x = gaussian * scaled**power_x
                filter_y = gaussian * scaled**power_y
                along_x.append(filter_x / np.sum(np.abs(filter_x)))
                along_y.append(filter_y / np.sum(np.abs(filter_y)))
    return np.stack(along_y), np.stack(along_x)


def transforms(extent):
    radius = KSIZE // 2
    length = extent + 2 * radius
    main = extent // 2
    low = np.arange(main)
    high = np.arange(main, length // 2 + 1)
    extra = high.size
    step = 2.0 * np.pi / length

    def trig(points, freqs):
        angle = step * np.outer(points, freqs)
        return np.cos(angle), np.sin(angle)

    def packed(first, second):
        out = np.zeros((first.shape[0], LANES))
        out[:, :extra] = first
        out[:, extra : 2 * extra] = second
        return out

    pixels = np.arange(extent)
    taps = np.arange(KSIZE) - radius
    cos_low, sin_low = trig(pixels, low)
    cos_high, sin_high = trig(pixels, high)
    forward = np.concatenate(
        [cos_low, sin_low, packed(cos_high, sin_high), packed(sin_high, cos_high)], 1
    )
    gain_low = np.where(low == 0, 1.0, 2.0) / length
    gain_high = np.where(high == length // 2, 1.0, 2.0) / length
    inverse = np.concatenate(
        [cos_low * gain_low, sin_low * gain_low, packed(cos_high * gain_high, sin_high * gain_high)],
        1,
    ).T
    tap_cos_low, tap_sin_low = trig(taps, low)
    tap_cos_high, tap_sin_high = trig(taps, high)
    tap_lanes = np.concatenate(
        [
            tap_cos_low,
            tap_sin_low,
            packed(tap_cos_high, tap_cos_high),
            packed(tap_sin_high, -tap_sin_high),
        ],
        1,
    )
    return (
        forward.astype(np.float32),
        np.ascontiguousarray(inverse).astype(np.float32),
        tap_lanes,
    )


def place_kernel(
    patch,
    pick,
    coef,
    corner,
    fill,
    exp_ref,
    var_ref,
    table_ref,
    forward_ref,
    inverse_ref,
    numer_in,
    denom_in,
    numer_out,
    denom_out,
    spectrum,
    product,
    numer_acc,
    denom_acc,
):
    step = pl.program_id(0)
    extent = exp_ref.shape[-1]
    groups = spectrum.shape[0]
    half = (groups - 2) // 2
    radius = KSIZE // 2

    @pl.when(step == 0)
    def _():
        numer_acc[:patch, :] = numer_in[...]
        denom_acc[:patch, :] = denom_in[...]
        blank = jnp.zeros((8, patch), jnp.float32)
        numer_acc[patch:, :] = blank
        denom_acc[patch:, :] = blank
        edge = jnp.zeros((groups, LEAD, LANES), jnp.float32)
        spectrum[:, :LEAD, :] = edge
        spectrum[:, LEAD + extent :, :] = edge

    lines = jnp.dot(
        exp_ref[0, 0], forward_ref[...], precision=HIGHEST, preferred_element_type=jnp.float32
    )
    for group in range(groups):
        spectrum[group, LEAD : LEAD + extent, :] = lines[:, group * LANES : (group + 1) * LANES]

    def taps_of(tap, group):
        return table_ref[0, tap : tap + 1, group * LANES : (group + 1) * LANES]

    for base in range(0, extent, ROWS):
        for group in range(half):
            real = jnp.zeros((ROWS, LANES), jnp.float32)
            imag = jnp.zeros((ROWS, LANES), jnp.float32)
            for tap in range(KSIZE):
                at = base + tap + LEAD - radius
                cosine = spectrum[group, at : at + ROWS, :]
                sine = spectrum[half + group, at : at + ROWS, :]
                tap_cos = taps_of(tap, group)
                tap_sin = taps_of(tap, half + group)
                real = real + tap_cos * cosine + tap_sin * sine
                imag = imag + tap_cos * sine - tap_sin * cosine
            product[base : base + ROWS, group * LANES : (group + 1) * LANES] = real
            product[
                base : base + ROWS, (half + group) * LANES : (half + group + 1) * LANES
            ] = imag
        both = jnp.zeros((ROWS, LANES), jnp.float32)
        for tap in range(KSIZE):
            at = base + tap + LEAD - radius
            both = (
                both
                + taps_of(tap, groups - 2) * spectrum[groups - 2, at : at + ROWS, :]
                + taps_of(tap, groups - 1) * spectrum[groups - 1, at : at + ROWS, :]
            )
        product[base : base + ROWS, (groups - 2) * LANES :] = both

    matched = jnp.dot(
        product[...], inverse_ref[...], precision=HIGHEST, preferred_element_type=jnp.float32
    )
    weight = fill[step].astype(jnp.float32) / var_ref[0, 0]
    row, col = corner[2 * step], corner[2 * step + 1]
    low_row = lax.rem(row, 8)
    first = pl.multiple_of(row - low_row, 8)

    def placed(tile):
        wide = jnp.concatenate([tile, jnp.zeros((extent, patch - extent), jnp.float32)], 1)
        wide = pltpu.roll(wide, col, 1)
        wide = jnp.concatenate([wide, jnp.zeros((8, patch), jnp.float32)], 0)
        return pltpu.roll(wide, low_row, 0)

    where = pl.ds(first, extent + 8)
    numer_acc[where, :] = numer_acc[where, :] + placed(weight * matched)
    denom_acc[where, :] = denom_acc[where, :] + placed(weight)

    @pl.when(step == pl.num_programs(0) - 1)
    def _():
        numer_out[...] = numer_acc[:patch, :]
        denom_out[...] = denom_acc[:patch, :]


def place_tiles(canvases, tiles, variance, plane, pick, about, tables, forward, inverse):
    coef, corner, fill = about
    patch = canvases[0].shape[0]
    extent = tiles.shape[-1]
    lanes = forward.shape[1]
    count = pick.shape[0]

    def whole(*shape):
        return pl.BlockSpec(shape, lambda i, *refs: (0,) * len(shape))

    def tile_spec(which):
        return pl.BlockSpec(
            (1, 1, extent, extent), lambda i, pick, *refs: (which, pick[i], 0, 0)
        )

    grid_spec = pltpu.PrefetchScalarGridSpec(
        num_scalar_prefetch=4,
        grid=(count,),
        in_specs=[
            tile_spec(0),
            tile_spec(plane),
            pl.BlockSpec((1, KSIZE, lanes), lambda i, pick, coef, *refs: (coef[i], 0, 0)),
            whole(*forward.shape),
            whole(*inverse.shape),
            whole(patch, patch),
            whole(patch, patch),
        ],
        out_specs=[whole(patch, patch), whole(patch, patch)],
        scratch_shapes=[
            pltpu.VMEM((lanes // LANES, extent + 2 * LEAD, LANES), jnp.float32),
            pltpu.VMEM((extent, lanes - LANES), jnp.float32),
            pltpu.VMEM((patch + 8, patch), jnp.float32),
            pltpu.VMEM((patch + 8, patch), jnp.float32),
        ],
    )
    return pl.pallas_call(
        functools.partial(place_kernel, patch),
        grid_spec=grid_spec,
        out_shape=[jax.ShapeDtypeStruct((patch, patch), jnp.float32)] * 2,
        compiler_params=pltpu.CompilerParams(
            vmem_limit_bytes=40 * 2**20
        ),
        cost_estimate=pl.CostEstimate(
            flops=count * 12 * extent * extent * lanes,
            bytes_accessed=16 * patch * patch + count * 8 * extent * extent,
            transcendentals=0,
        ),
    )(pick, coef, corner.reshape(-1), fill, tiles, variance, tables, forward, inverse, *canvases)


def gather_kernel(pick, exp_ref, var_ref, out_ref):
    out_ref[0] = exp_ref[...]
    out_ref[1] = var_ref[...]


def gather_tiles(tiles, variance, pick):
    extent = tiles.shape[-1]
    count = pick.shape[0]
    tile_spec = pl.BlockSpec((1, extent, extent), lambda i, pick: (pick[i], 0, 0))
    return pl.pallas_call(
        gather_kernel,
        grid_spec=pltpu.PrefetchScalarGridSpec(
            num_scalar_prefetch=1,
            grid=(count,),
            in_specs=[tile_spec, tile_spec],
            out_specs=pl.BlockSpec((2, 1, extent, extent), lambda i, pick: (0, i, 0, 0)),
        ),
        out_shape=jax.ShapeDtypeStruct((2, count, extent, extent), jnp.float32),
        compiler_params=pltpu.CompilerParams(vmem_limit_bytes=16 * 2**20),
        cost_estimate=pl.CostEstimate(
            flops=0, bytes_accessed=16 * count * extent * extent, transcendentals=0
        ),
    )(pick, tiles, variance)


def band(taps, outputs):
    size = taps.shape[0]
    shape = (outputs + size - 1, outputs)
    lag = lax.broadcasted_iota(jnp.int32, shape, 0) - lax.broadcasted_iota(jnp.int32, shape, 1)
    out = jnp.zeros(shape, jnp.float32)
    for tap in range(size):
        out = jnp.where(lag == tap, taps[tap], out)
    return out


def shifted(value, sky_step, src_step):
    skies, owners = lax.axis_size("sky"), lax.axis_size("src")
    pairs = []
    for sky in range(skies):
        for src in range(owners):
            to = src + src_step
            if 0 <= to < owners:
                target = ((sky + sky_step) % skies) * owners + to
                pairs.append((sky * owners + src, target))
    return lax.ppermute(value, ("sky", "src"), pairs)


def on_device(
    exposures, variance, coef_table, coef_index, offsets, tile_codes, detect_ra, detect_dec
):
    owners = lax.axis_size("src")
    me = lax.axis_index("src")
    tiles, variances = exposures[0], variance[0]
    count, extent = tiles.shape[0], tiles.shape[-1]
    patch = 2 * extent
    codes_here = tile_codes[0]
    entries = jnp.arange(count, dtype=jnp.int32)

    def ranks(codes):
        same = codes[..., :, None] == codes[..., None, :]
        earlier = entries[None, :] < entries[:, None]
        return jnp.sum((same & earlier).astype(jnp.int32), -1)

    def slots(codes, wanted):
        match = (codes == wanted)[..., None, :] & (
            ranks(codes)[..., None, :] == jnp.arange(CAP, dtype=jnp.int32)[:, None]
        )
        return match.astype(jnp.int32)

    wanted_codes = jnp.arange(2 * owners, dtype=jnp.int32)[:, None]
    chooser = slots(jnp.broadcast_to(codes_here, (2 * owners, count)), wanted_codes)
    source = jnp.sum(chooser * entries, -1).reshape(2, owners, CAP)

    about = jnp.concatenate([codes_here[:, None], coef_index[0][:, None], offsets[0]], 1)
    everyone = lax.all_gather(about, "src")
    codes_all = everyone[:, :, 0]
    got = jnp.stack([slots(codes_all, r * owners + me) for r in range(2)])
    fill = jnp.sum(got, -1)
    coef = jnp.sum(got * everyone[None, :, None, :, 1], -1)
    corner = jnp.stack([jnp.sum(got * everyone[None, :, None, :, 2 + d], -1) for d in range(2)], -1)

    forward, inverse, tap_lanes = transforms(extent)
    along_y, along_x = basis_filters()
    lanes_x = (along_x @ tap_lanes).astype(np.float32)
    basis = jnp.asarray(along_y.astype(np.float32))[:, :, None] * jnp.asarray(lanes_x)[:, None, :]
    tables = jnp.einsum(
        "ck,ksl->csl", coef_table, basis, precision=HIGHEST, preferred_element_type=jnp.float32
    )
    forward, inverse = jnp.asarray(forward), jnp.asarray(inverse)

    def send(row_step, partner, after):
        picks = lax.dynamic_index_in_dim(source[row_step], me ^ partner, 0, keepdims=False)
        out = gather_tiles(tiles, variances, picks)
        if after is not None:
            out, after = lax.optimization_barrier((out, after))
        pairs = [(i, i ^ partner) for i in range(owners)]
        return lax.ppermute(out, "src", pairs), after

    def add(canvases, row_step, partner, held):
        def of(value):
            return lax.dynamic_index_in_dim(value, me ^ partner, 0, keepdims=False)

        if held is None:
            picks = of(source[row_step])
            held, spread, plane = tiles[None], variances[None], 0
        else:
            spread, plane = held, 1
            picks = jnp.arange(CAP, dtype=jnp.int32)
        notes = (of(coef[row_step]), of(corner[row_step]), of(fill[row_step]))
        return place_tiles(
            canvases, held, spread, plane, picks, notes, tables, forward, inverse
        )

    zero = jnp.zeros((patch, patch), jnp.float32)
    far = range(2, owners)
    arrived = {}
    for partner in far:
        arrived[1, partner], _ = send(1, partner, None)
    arrived[1, 1], _ = send(1, 1, None)
    arrived[0, 1], _ = send(0, 1, None)
    for partner in far:
        arrived[0, partner], arrived[1, partner] = send(0, partner, arrived[1, partner])

    ahead = (zero, zero)
    ahead = add(ahead, 1, 0, None)
    ahead = add(ahead, 1, 1, arrived[1, 1])
    here = add((zero, zero), 0, 0, None)
    here = add(here, 0, 1, arrived[0, 1])
    for partner in far:
        ahead = add(ahead, 1, partner, arrived[1, partner])
    moved = [shifted(value, 1, 0) for value in ahead]
    for partner in far:
        here = add(here, 0, partner, arrived[0, partner])
    coadd = (here[0] + moved[0]) / (here[1] + moved[1] + 1.0)

    rim = detect_ra.shape[0] // 2
    along_dec = band(detect_dec, patch)
    along_ra = band(detect_ra, patch).T
    top, bottom = coadd[:rim], coadd[patch - rim :]

    def widened(rows, sky_step):
        return jnp.concatenate(
            [
                shifted(rows[:, patch - rim :], sky_step, 1),
                shifted(rows, sky_step, 0) if sky_step else rows,
                shifted(rows[:, :rim], sky_step, -1),
            ],
            1,
        )

    extended = jnp.concatenate([widened(bottom, 1), widened(coadd, 0), widened(top, -1)], 0)
    dot = functools.partial(jnp.dot, precision=HIGHEST, preferred_element_type=jnp.float32)
    detection = dot(along_ra, dot(extended, along_dec))
    return (coadd, detection)


def solution(mesh):
    return jax.shard_map(
        on_device,
        mesh=mesh,
        in_specs=(
            P("sky", "src", None, None),
            P("sky", "src", None, None),
            P(),
            P("sky", "src"),
            P("sky", "src", None),
            P("sky", "src"),
            P(),
            P(),
        ),
        out_specs=(P("sky", "src"), P("sky", "src")),
        check_vma=False,
    )
```

```python
import functools

import ml_dtypes
import numpy as np
import jax
import jax.numpy as jnp
from jax import lax
from jax.experimental import pallas as pl
from jax.experimental.pallas import tpu as pltpu
from jax.sharding import PartitionSpec as P

CAP = 2
KSIZE = 21
SPREADS = (0.75, 1.5, 3.0)
LANES = 128
LEAD = 16
ROWS = 64
VMEM = 60 * 2**20
HIGHEST = lax.Precision.HIGHEST


def halves(value):
    high = value.astype(jnp.bfloat16)
    return high, (value - high.astype(jnp.float32)).astype(jnp.bfloat16)


def product_of(left, right):
    dot = functools.partial(jnp.dot, preferred_element_type=jnp.float32)
    return dot(left[1], right[0]) + dot(left[0], right[1]) + dot(left[0], right[0])


def basis_filters():
    centred = np.arange(KSIZE, dtype=np.float64) - KSIZE // 2
    along_x, along_y = [], []
    for spread in SPREADS:
        gaussian = np.exp(-(centred * centred) / (2.0 * spread * spread))
        scaled = centred / spread
        for power_x in range(5):
            for power_y in range(5 - power_x):
                filter_x = gaussian * scaled**power_x
                filter_y = gaussian * scaled**power_y
                along_x.append(filter_x / np.sum(np.abs(filter_x)))
                along_y.append(filter_y / np.sum(np.abs(filter_y)))
    return np.stack(along_y), np.stack(along_x)


def transforms(extent):
    radius = KSIZE // 2
    length = extent + 2 * radius
    main = extent // 2
    low = np.arange(main)
    high = np.arange(main, length // 2 + 1)
    extra = high.size
    step = 2.0 * np.pi / length

    def trig(points, freqs):
        angle = step * np.outer(points, freqs)
        return np.cos(angle), np.sin(angle)

    def packed(first, second):
        out = np.zeros((first.shape[0], LANES))
        out[:, :extra] = first
        out[:, extra : 2 * extra] = second
        return out

    pixels = np.arange(extent)
    taps = np.arange(KSIZE) - radius
    cos_low, sin_low = trig(pixels, low)
    cos_high, sin_high = trig(pixels, high)
    forward = np.concatenate(
        [cos_low, sin_low, packed(cos_high, sin_high), packed(sin_high, cos_high)], 1
    )
    gain_low = np.where(low == 0, 1.0, 2.0) / length
    gain_high = np.where(high == length // 2, 1.0, 2.0) / length
    inverse = np.concatenate(
        [cos_low * gain_low, sin_low * gain_low, packed(cos_high * gain_high, sin_high * gain_high)],
        1,
    ).T
    tap_cos_low, tap_sin_low = trig(taps, low)
    tap_cos_high, tap_sin_high = trig(taps, high)
    tap_lanes = np.concatenate(
        [
            tap_cos_low,
            tap_sin_low,
            packed(tap_cos_high, tap_cos_high),
            packed(tap_sin_high, -tap_sin_high),
        ],
        1,
    )
    def split(matrix):
        high = matrix.astype(ml_dtypes.bfloat16)
        return np.stack([high, (matrix - high.astype(np.float64)).astype(ml_dtypes.bfloat16)])

    return split(forward), split(inverse), tap_lanes


def place_kernel(
    patch,
    pick,
    coef,
    corner,
    fill,
    exp_ref,
    var_ref,
    table_ref,
    forward_ref,
    inverse_ref,
    numer_in,
    denom_in,
    numer_out,
    denom_out,
    spectrum,
    product,
    numer_acc,
    denom_acc,
):
    step = pl.program_id(0)
    extent = exp_ref.shape[-1]
    groups = spectrum.shape[0]
    half = (groups - 2) // 2
    radius = KSIZE // 2

    @pl.when(step == 0)
    def _():
        numer_acc[:patch, :] = numer_in[...]
        denom_acc[:patch, :] = denom_in[...]
        blank = jnp.zeros((8, patch), jnp.float32)
        numer_acc[patch:, :] = blank
        denom_acc[patch:, :] = blank
        edge = jnp.zeros((groups, LEAD, LANES), jnp.float32)
        spectrum[:, :LEAD, :] = edge
        spectrum[:, LEAD + extent :, :] = edge

    lines = product_of(halves(exp_ref[0, 0]), (forward_ref[0], forward_ref[1]))
    for group in range(groups):
        spectrum[group, LEAD : LEAD + extent, :] = lines[:, group * LANES : (group + 1) * LANES]

    def taps_of(tap, group):
        return table_ref[0, tap : tap + 1, group * LANES : (group + 1) * LANES]

    for base in range(0, extent, ROWS):
        for group in range(half):
            real = jnp.zeros((ROWS, LANES), jnp.float32)
            imag = jnp.zeros((ROWS, LANES), jnp.float32)
            for tap in range(KSIZE):
                at = base + tap + LEAD - radius
                cosine = spectrum[group, at : at + ROWS, :]
                sine = spectrum[half + group, at : at + ROWS, :]
                tap_cos = taps_of(tap, group)
                tap_sin = taps_of(tap, half + group)
                real = real + tap_cos * cosine + tap_sin * sine
                imag = imag + tap_cos * sine - tap_sin * cosine
            product[base : base + ROWS, group * LANES : (group + 1) * LANES] = real
            product[
                base : base + ROWS, (half + group) * LANES : (half + group + 1) * LANES
            ] = imag
        both = jnp.zeros((ROWS, LANES), jnp.float32)
        for tap in range(KSIZE):
            at = base + tap + LEAD - radius
            both = (
                both
                + taps_of(tap, groups - 2) * spectrum[groups - 2, at : at + ROWS, :]
                + taps_of(tap, groups - 1) * spectrum[groups - 1, at : at + ROWS, :]
            )
        product[base : base + ROWS, (groups - 2) * LANES :] = both

    matched = product_of(halves(product[...]), (inverse_ref[0], inverse_ref[1]))
    weight = fill[step].astype(jnp.float32) / var_ref[0, 0]
    row, col = corner[2 * step], corner[2 * step + 1]
    low_row = lax.rem(row, 8)
    first = pl.multiple_of(row - low_row, 8)

    def placed(tile):
        wide = jnp.concatenate([tile, jnp.zeros((extent, patch - extent), jnp.float32)], 1)
        wide = pltpu.roll(wide, col, 1)
        wide = jnp.concatenate([wide, jnp.zeros((8, patch), jnp.float32)], 0)
        return pltpu.roll(wide, low_row, 0)

    where = pl.ds(first, extent + 8)
    numer_acc[where, :] = numer_acc[where, :] + placed(weight * matched)
    denom_acc[where, :] = denom_acc[where, :] + placed(weight)

    @pl.when(step == pl.num_programs(0) - 1)
    def _():
        numer_out[...] = numer_acc[:patch, :]
        denom_out[...] = denom_acc[:patch, :]


def place_tiles(canvases, tiles, variance, plane, pick, about, tables, forward, inverse):
    coef, corner, fill = about
    patch = canvases[0].shape[0]
    extent = tiles.shape[-1]
    lanes = forward.shape[-1]
    count = pick.shape[0]

    def whole(*shape):
        return pl.BlockSpec(shape, lambda i, *refs: (0,) * len(shape))

    def tile_spec(which):
        return pl.BlockSpec(
            (1, 1, extent, extent), lambda i, pick, *refs: (which, pick[i], 0, 0)
        )

    grid_spec = pltpu.PrefetchScalarGridSpec(
        num_scalar_prefetch=4,
        grid=(count,),
        in_specs=[
            tile_spec(0),
            tile_spec(plane),
            pl.BlockSpec((1, KSIZE, lanes), lambda i, pick, coef, *refs: (coef[i], 0, 0)),
            whole(*forward.shape),
            whole(*inverse.shape),
            whole(patch, patch),
            whole(patch, patch),
        ],
        out_specs=[whole(patch, patch), whole(patch, patch)],
        scratch_shapes=[
            pltpu.VMEM((lanes // LANES, extent + 2 * LEAD, LANES), jnp.float32),
            pltpu.VMEM((extent, lanes - LANES), jnp.float32),
            pltpu.VMEM((patch + 8, patch), jnp.float32),
            pltpu.VMEM((patch + 8, patch), jnp.float32),
        ],
    )
    return pl.pallas_call(
        functools.partial(place_kernel, patch),
        grid_spec=grid_spec,
        out_shape=[jax.ShapeDtypeStruct((patch, patch), jnp.float32)] * 2,
        compiler_params=pltpu.CompilerParams(
            vmem_limit_bytes=VMEM
        ),
        cost_estimate=pl.CostEstimate(
            flops=count * 80 * extent * extent * lanes,
            bytes_accessed=16 * patch * patch + count * 8 * extent * extent,
            transcendentals=0,
        ),
    )(pick, coef, corner.reshape(-1), fill, tiles, variance, tables, forward, inverse, *canvases)


def gather_kernel(pick, exp_ref, var_ref, out_ref):
    out_ref[0] = exp_ref[...]
    out_ref[1] = var_ref[...]


def gather_tiles(tiles, variance, pick):
    extent = tiles.shape[-1]
    count = pick.shape[0]
    tile_spec = pl.BlockSpec((1, extent, extent), lambda i, pick: (pick[i], 0, 0))
    return pl.pallas_call(
        gather_kernel,
        grid_spec=pltpu.PrefetchScalarGridSpec(
            num_scalar_prefetch=1,
            grid=(count,),
            in_specs=[tile_spec, tile_spec],
            out_specs=pl.BlockSpec((2, 1, extent, extent), lambda i, pick: (0, i, 0, 0)),
        ),
        out_shape=jax.ShapeDtypeStruct((2, count, extent, extent), jnp.float32),
        compiler_params=pltpu.CompilerParams(vmem_limit_bytes=VMEM),
        cost_estimate=pl.CostEstimate(
            flops=0, bytes_accessed=16 * count * extent * extent, transcendentals=0
        ),
    )(pick, tiles, variance)


def band(taps, outputs):
    size = taps.shape[0]
    shape = (outputs + size - 1, outputs)
    lag = lax.broadcasted_iota(jnp.int32, shape, 0) - lax.broadcasted_iota(jnp.int32, shape, 1)
    out = jnp.zeros(shape, jnp.float32)
    for tap in range(size):
        out = jnp.where(lag == tap, taps[tap], out)
    return out


def inner_and_rims(matrix, rim, axis):
    size = matrix.shape[axis]
    cut = functools.partial(lax.slice_in_dim, matrix, axis=axis)
    return cut(rim, size - rim), jnp.concatenate([cut(0, rim), cut(size - rim, size)], axis)


def columns_kernel(rows_ref, edge_ref, middle_ref, edges_ref, out_ref):
    out_ref[...] = product_of(halves(rows_ref[...]), halves(middle_ref[...])) + product_of(
        halves(edge_ref[...]), halves(edges_ref[...])
    )


def rows_kernel(
    filtered_ref, near_ref, corner_ref, middle_ref, edges_ref, across_ref, rims_ref, out_ref
):
    outside = product_of(halves(near_ref[...]), halves(middle_ref[...])) + product_of(
        halves(corner_ref[...]), halves(edges_ref[...])
    )
    out_ref[...] = product_of(halves(across_ref[...]), halves(filtered_ref[...])) + product_of(
        halves(rims_ref[...]), halves(outside)
    )


def filter_call(kernel, *operands):
    return pl.pallas_call(
        kernel,
        out_shape=jax.ShapeDtypeStruct(operands[0].shape, jnp.float32),
        in_specs=[pl.BlockSpec(memory_space=pltpu.VMEM)] * len(operands),
        out_specs=pl.BlockSpec(memory_space=pltpu.VMEM),
        compiler_params=pltpu.CompilerParams(vmem_limit_bytes=VMEM),
        cost_estimate=pl.CostEstimate(
            flops=6 * operands[0].size * operands[0].shape[1],
            bytes_accessed=sum(4 * operand.size for operand in operands),
            transcendentals=0,
        ),
    )(*operands)


filter_columns = functools.partial(filter_call, columns_kernel)
filter_rows = functools.partial(filter_call, rows_kernel)


def shifted(value, sky_step, src_step):
    skies, owners = lax.axis_size("sky"), lax.axis_size("src")
    pairs = []
    for sky in range(skies):
        for src in range(owners):
            to = src + src_step
            if 0 <= to < owners:
                target = ((sky + sky_step) % skies) * owners + to
                pairs.append((sky * owners + src, target))
    return lax.ppermute(value, ("sky", "src"), pairs)


def on_device(
    exposures, variance, coef_table, coef_index, offsets, tile_codes, detect_ra, detect_dec
):
    owners = lax.axis_size("src")
    me = lax.axis_index("src")
    tiles, variances = exposures[0], variance[0]
    count, extent = tiles.shape[0], tiles.shape[-1]
    patch = 2 * extent
    codes_here = tile_codes[0]
    entries = jnp.arange(count, dtype=jnp.int32)

    same = codes_here[:, None] == codes_here[None, :]
    earlier = entries[None, :] < entries[:, None]
    rank = jnp.sum((same & earlier).astype(jnp.int32), -1)

    slot = jnp.arange(2 * owners * CAP, dtype=jnp.int32).reshape(2 * owners, CAP, 1)
    chooser = (codes_here * CAP + rank == slot).astype(jnp.int32)
    source = jnp.sum(chooser * entries, -1).reshape(2, owners, CAP)

    about = jnp.concatenate([coef_index[0][:, None], offsets[0]], 1)
    notes = jnp.sum(chooser[..., None] * about, 2)
    notes = jnp.concatenate([notes, jnp.sum(chooser, -1)[..., None]], -1)
    notes = notes.reshape(2, owners, CAP, 4)

    forward, inverse, tap_lanes = transforms(extent)
    along_y, along_x = basis_filters()
    lanes_x = (along_x @ tap_lanes).astype(np.float32)
    basis = jnp.asarray(along_y.astype(np.float32))[:, :, None] * jnp.asarray(lanes_x)[:, None, :]
    tables = jnp.einsum(
        "ck,ksl->csl", coef_table, basis, precision=HIGHEST, preferred_element_type=jnp.float32
    )
    forward, inverse = jnp.asarray(forward), jnp.asarray(inverse)

    def swapped(value, partner):
        return lax.ppermute(value, "src", [(i, i ^ partner) for i in range(owners)])

    def towards(value, partner, axis=0):
        return lax.dynamic_index_in_dim(value, me ^ partner, axis, keepdims=False)

    told = {partner: swapped(towards(notes, partner, 1), partner) for partner in range(1, owners)}
    told[0] = towards(notes, 0, 1)

    def send(row_step, partner, after):
        picks = towards(source[row_step], partner)
        out = gather_tiles(tiles, variances, picks)
        if after is not None:
            out, after = lax.optimization_barrier((out, after))
        return swapped(out, partner), after

    def add(canvases, row_step, partner, held):
        if held is None:
            picks = towards(source[row_step], 0)
            held, spread, plane = tiles[None], variances[None], 0
        else:
            spread, plane = held, 1
            picks = jnp.arange(CAP, dtype=jnp.int32)
        note = told[partner][row_step]
        note = (note[:, 0], note[:, 1:3], note[:, 3])
        return place_tiles(
            canvases, held, spread, plane, picks, note, tables, forward, inverse
        )

    zero = jnp.zeros((patch, patch), jnp.float32)
    far = range(2, owners)
    arrived = {}
    for partner in far:
        arrived[1, partner], _ = send(1, partner, None)
    arrived[1, 1], _ = send(1, 1, None)
    arrived[0, 1], _ = send(0, 1, None)
    for partner in far:
        arrived[0, partner], arrived[1, partner] = send(0, partner, arrived[1, partner])

    ahead = (zero, zero)
    ahead = add(ahead, 1, 0, None)
    ahead = add(ahead, 1, 1, arrived[1, 1])
    here = add((zero, zero), 0, 0, None)
    here = add(here, 0, 1, arrived[0, 1])
    ahead, here = lax.optimization_barrier((ahead, here))
    for partner in far:
        ahead = add(ahead, 1, partner, arrived[1, partner])
    moved = [shifted(value, 1, 0) for value in ahead]
    for partner in far:
        here = add(here, 0, partner, arrived[0, partner])
    coadd = (here[0] + moved[0]) / (here[1] + moved[1] + 1.0)

    rim = detect_ra.shape[0] // 2
    along_dec = band(detect_dec, patch)
    along_ra = band(detect_ra, patch).T
    left = shifted(coadd[:, patch - rim :], 0, 1)
    right = shifted(coadd[:, :rim], 0, -1)

    def rows(first):
        return jnp.concatenate([part[first : first + rim] for part in (coadd, left, right)], 1)

    near = jnp.concatenate([shifted(rows(patch - rim), 1, 0), shifted(rows(0), -1, 0)], 0)
    middle, edges = inner_and_rims(along_dec, rim, 0)
    filtered = filter_columns(coadd, jnp.concatenate([left, right], 1), middle, edges)
    detection = filter_rows(
        filtered,
        near[:, :patch],
        near[:, patch:],
        middle,
        edges,
        *inner_and_rims(along_ra, rim, 1),
    )
    return (coadd, detection)


def solution(mesh):
    return jax.shard_map(
        on_device,
        mesh=mesh,
        in_specs=(
            P("sky", "src", None, None),
            P("sky", "src", None, None),
            P(),
            P("sky", "src"),
            P("sky", "src", None),
            P("sky", "src"),
            P(),
            P(),
        ),
        out_specs=(P("sky", "src"), P("sky", "src")),
        check_vma=False,
    )
```

```python
import functools

import ml_dtypes
import numpy as np
import jax
import jax.numpy as jnp
from jax import lax
from jax.experimental import pallas as pl
from jax.experimental.pallas import tpu as pltpu
from jax.sharding import PartitionSpec as P

CAP = 2
KSIZE = 21
SPREADS = (0.75, 1.5, 3.0)
LANES = 128
LEAD = 16
ROWS = 64
VMEM = 60 * 2**20
HIGHEST = lax.Precision.HIGHEST


def halves(value):
    high = value.astype(jnp.bfloat16)
    return high, (value - high.astype(jnp.float32)).astype(jnp.bfloat16)


def product_of(left, right):
    dot = functools.partial(jnp.dot, preferred_element_type=jnp.float32)
    return dot(left[1], right[0]) + dot(left[0], right[1]) + dot(left[0], right[0])


def basis_filters():
    centred = np.arange(KSIZE, dtype=np.float64) - KSIZE // 2
    along_x, along_y = [], []
    for spread in SPREADS:
        gaussian = np.exp(-(centred * centred) / (2.0 * spread * spread))
        scaled = centred / spread
        for power_x in range(5):
            for power_y in range(5 - power_x):
                filter_x = gaussian * scaled**power_x
                filter_y = gaussian * scaled**power_y
                along_x.append(filter_x / np.sum(np.abs(filter_x)))
                along_y.append(filter_y / np.sum(np.abs(filter_y)))
    return np.stack(along_y), np.stack(along_x)


def transforms(extent):
    radius = KSIZE // 2
    length = extent + 2 * radius
    main = extent // 2
    low = np.arange(main)
    high = np.arange(main, length // 2 + 1)
    extra = high.size
    step = 2.0 * np.pi / length

    def trig(points, freqs):
        angle = step * np.outer(points, freqs)
        return np.cos(angle), np.sin(angle)

    def packed(first, second):
        out = np.zeros((first.shape[0], LANES))
        out[:, :extra] = first
        out[:, extra : 2 * extra] = second
        return out

    pixels = np.arange(extent)
    taps = np.arange(KSIZE) - radius
    cos_low, sin_low = trig(pixels, low)
    cos_high, sin_high = trig(pixels, high)
    forward = np.concatenate(
        [cos_low, sin_low, packed(cos_high, sin_high), packed(sin_high, cos_high)], 1
    )
    gain_low = np.where(low == 0, 1.0, 2.0) / length
    gain_high = np.where(high == length // 2, 1.0, 2.0) / length
    inverse = np.concatenate(
        [cos_low * gain_low, sin_low * gain_low, packed(cos_high * gain_high, sin_high * gain_high)],
        1,
    ).T
    tap_cos_low, tap_sin_low = trig(taps, low)
    tap_cos_high, tap_sin_high = trig(taps, high)
    tap_lanes = np.concatenate(
        [
            tap_cos_low,
            tap_sin_low,
            packed(tap_cos_high, tap_cos_high),
            packed(tap_sin_high, -tap_sin_high),
        ],
        1,
    )
    def split(matrix):
        high = matrix.astype(ml_dtypes.bfloat16)
        return np.stack([high, (matrix - high.astype(np.float64)).astype(ml_dtypes.bfloat16)])

    return split(forward), split(inverse), tap_lanes


def place_kernel(
    patch,
    pick,
    coef,
    corner,
    fill,
    exp_ref,
    var_ref,
    table_ref,
    forward_ref,
    inverse_ref,
    numer_in,
    denom_in,
    numer_out,
    denom_out,
    spectrum,
    product,
    numer_acc,
    denom_acc,
):
    step = pl.program_id(0)
    extent = exp_ref.shape[-1]
    groups = spectrum.shape[0]
    half = (groups - 2) // 2
    radius = KSIZE // 2

    @pl.when(step == 0)
    def _():
        numer_acc[:patch, :] = numer_in[...]
        denom_acc[:patch, :] = denom_in[...]
        blank = jnp.zeros((8, patch), jnp.float32)
        numer_acc[patch:, :] = blank
        denom_acc[patch:, :] = blank
        edge = jnp.zeros((groups, LEAD, LANES), jnp.float32)
        spectrum[:, :LEAD, :] = edge
        spectrum[:, LEAD + extent :, :] = edge

    lines = product_of(halves(exp_ref[0, 0]), (forward_ref[0], forward_ref[1]))
    for group in range(groups):
        spectrum[group, LEAD : LEAD + extent, :] = lines[:, group * LANES : (group + 1) * LANES]

    def taps_of(tap, group):
        return table_ref[0, tap : tap + 1, group * LANES : (group + 1) * LANES]

    for base in range(0, extent, ROWS):
        for group in range(half):
            real = jnp.zeros((ROWS, LANES), jnp.float32)
            imag = jnp.zeros((ROWS, LANES), jnp.float32)
            for tap in range(KSIZE):
                at = base + tap + LEAD - radius
                cosine = spectrum[group, at : at + ROWS, :]
                sine = spectrum[half + group, at : at + ROWS, :]
                tap_cos = taps_of(tap, group)
                tap_sin = taps_of(tap, half + group)
                real = real + tap_cos * cosine + tap_sin * sine
                imag = imag + tap_cos * sine - tap_sin * cosine
            product[base : base + ROWS, group * LANES : (group + 1) * LANES] = real
            product[
                base : base + ROWS, (half + group) * LANES : (half + group + 1) * LANES
            ] = imag
        both = jnp.zeros((ROWS, LANES), jnp.float32)
        for tap in range(KSIZE):
            at = base + tap + LEAD - radius
            both = (
                both
                + taps_of(tap, groups - 2) * spectrum[groups - 2, at : at + ROWS, :]
                + taps_of(tap, groups - 1) * spectrum[groups - 1, at : at + ROWS, :]
            )
        product[base : base + ROWS, (groups - 2) * LANES :] = both

    matched = product_of(halves(product[...]), (inverse_ref[0], inverse_ref[1]))
    weight = fill[step].astype(jnp.float32) / var_ref[0, 0]
    row, col = corner[2 * step], corner[2 * step + 1]
    low_row = lax.rem(row, 8)
    first = pl.multiple_of(row - low_row, 8)

    def placed(tile):
        wide = jnp.concatenate([tile, jnp.zeros((extent, patch - extent), jnp.float32)], 1)
        wide = pltpu.roll(wide, col, 1)
        wide = jnp.concatenate([wide, jnp.zeros((8, patch), jnp.float32)], 0)
        return pltpu.roll(wide, low_row, 0)

    where = pl.ds(first, extent + 8)
    numer_acc[where, :] = numer_acc[where, :] + placed(weight * matched)
    denom_acc[where, :] = denom_acc[where, :] + placed(weight)

    @pl.when(step == pl.num_programs(0) - 1)
    def _():
        numer_out[...] = numer_acc[:patch, :]
        denom_out[...] = denom_acc[:patch, :]


def place_tiles(canvases, tiles, variance, plane, pick, about, tables, forward, inverse):
    coef, corner, fill = about
    patch = canvases[0].shape[0]
    extent = tiles.shape[-1]
    lanes = forward.shape[-1]
    count = pick.shape[0]

    def whole(*shape):
        return pl.BlockSpec(shape, lambda i, *refs: (0,) * len(shape))

    def tile_spec(which):
        return pl.BlockSpec(
            (1, 1, extent, extent), lambda i, pick, *refs: (which, pick[i], 0, 0)
        )

    grid_spec = pltpu.PrefetchScalarGridSpec(
        num_scalar_prefetch=4,
        grid=(count,),
        in_specs=[
            tile_spec(0),
            tile_spec(plane),
            pl.BlockSpec((1, KSIZE, lanes), lambda i, pick, coef, *refs: (coef[i], 0, 0)),
            whole(*forward.shape),
            whole(*inverse.shape),
            whole(patch, patch),
            whole(patch, patch),
        ],
        out_specs=[whole(patch, patch), whole(patch, patch)],
        scratch_shapes=[
            pltpu.VMEM((lanes // LANES, extent + 2 * LEAD, LANES), jnp.float32),
            pltpu.VMEM((extent, lanes - LANES), jnp.float32),
            pltpu.VMEM((patch + 8, patch), jnp.float32),
            pltpu.VMEM((patch + 8, patch), jnp.float32),
        ],
    )
    return pl.pallas_call(
        functools.partial(place_kernel, patch),
        grid_spec=grid_spec,
        out_shape=[jax.ShapeDtypeStruct((patch, patch), jnp.float32)] * 2,
        compiler_params=pltpu.CompilerParams(
            vmem_limit_bytes=VMEM
        ),
        cost_estimate=pl.CostEstimate(
            flops=count * 80 * extent * extent * lanes,
            bytes_accessed=16 * patch * patch + count * 8 * extent * extent,
            transcendentals=0,
        ),
    )(pick, coef, corner.reshape(-1), fill, tiles, variance, tables, forward, inverse, *canvases)


def gather_kernel(pick, exp_ref, var_ref, out_ref):
    out_ref[0] = exp_ref[...]
    out_ref[1] = var_ref[...]


def gather_tiles(tiles, variance, pick):
    extent = tiles.shape[-1]
    count = pick.shape[0]
    tile_spec = pl.BlockSpec((1, extent, extent), lambda i, pick: (pick[i], 0, 0))
    return pl.pallas_call(
        gather_kernel,
        grid_spec=pltpu.PrefetchScalarGridSpec(
            num_scalar_prefetch=1,
            grid=(count,),
            in_specs=[tile_spec, tile_spec],
            out_specs=pl.BlockSpec((2, 1, extent, extent), lambda i, pick: (0, i, 0, 0)),
        ),
        out_shape=jax.ShapeDtypeStruct((2, count, extent, extent), jnp.float32),
        compiler_params=pltpu.CompilerParams(vmem_limit_bytes=VMEM),
        cost_estimate=pl.CostEstimate(
            flops=0, bytes_accessed=16 * count * extent * extent, transcendentals=0
        ),
    )(pick, tiles, variance)


def band_kernel(taps_ref, out_ref):
    spread = jnp.broadcast_to(taps_ref[...], out_ref.shape)
    out_ref[...] = pltpu.roll(spread, 0, 1, stride=1, stride_axis=0)


def band(taps, outputs):
    size = taps.shape[0]
    width = outputs + LANES
    row = jnp.concatenate([taps, jnp.zeros((width - size,), jnp.float32)])[None]
    wide = pl.pallas_call(
        band_kernel,
        out_shape=jax.ShapeDtypeStruct((outputs, width), jnp.float32),
        in_specs=[pl.BlockSpec(memory_space=pltpu.VMEM)],
        out_specs=pl.BlockSpec(memory_space=pltpu.VMEM),
        compiler_params=pltpu.CompilerParams(vmem_limit_bytes=VMEM),
    )(row)
    return wide[:, : outputs + size - 1]


def inner_and_rims(matrix, rim, axis):
    size = matrix.shape[axis]
    cut = functools.partial(lax.slice_in_dim, matrix, axis=axis)
    return cut(rim, size - rim), jnp.concatenate([cut(0, rim), cut(size - rim, size)], axis)


def columns_kernel(rows_ref, edge_ref, middle_ref, edges_ref, out_ref):
    out_ref[...] = product_of(halves(rows_ref[...]), halves(middle_ref[...])) + product_of(
        halves(edge_ref[...]), halves(edges_ref[...])
    )


def rows_kernel(
    filtered_ref, near_ref, corner_ref, middle_ref, edges_ref, across_ref, rims_ref, out_ref
):
    outside = product_of(halves(near_ref[...]), halves(middle_ref[...])) + product_of(
        halves(corner_ref[...]), halves(edges_ref[...])
    )
    out_ref[...] = product_of(halves(across_ref[...]), halves(filtered_ref[...])) + product_of(
        halves(rims_ref[...]), halves(outside)
    )


def filter_call(kernel, *operands):
    return pl.pallas_call(
        kernel,
        out_shape=jax.ShapeDtypeStruct(operands[0].shape, jnp.float32),
        in_specs=[pl.BlockSpec(memory_space=pltpu.VMEM)] * len(operands),
        out_specs=pl.BlockSpec(memory_space=pltpu.VMEM),
        compiler_params=pltpu.CompilerParams(vmem_limit_bytes=VMEM),
        cost_estimate=pl.CostEstimate(
            flops=6 * operands[0].size * operands[0].shape[1],
            bytes_accessed=sum(4 * operand.size for operand in operands),
            transcendentals=0,
        ),
    )(*operands)


filter_columns = functools.partial(filter_call, columns_kernel)
filter_rows = functools.partial(filter_call, rows_kernel)


def shifted(value, sky_step, src_step):
    skies, owners = lax.axis_size("sky"), lax.axis_size("src")
    pairs = []
    for sky in range(skies):
        for src in range(owners):
            to = src + src_step
            if 0 <= to < owners:
                target = ((sky + sky_step) % skies) * owners + to
                pairs.append((sky * owners + src, target))
    return lax.ppermute(value, ("sky", "src"), pairs)


def on_device(
    exposures, variance, coef_table, coef_index, offsets, tile_codes, detect_ra, detect_dec
):
    owners = lax.axis_size("src")
    me = lax.axis_index("src")
    tiles, variances = exposures[0], variance[0]
    count, extent = tiles.shape[0], tiles.shape[-1]
    patch = 2 * extent
    codes_here = tile_codes[0]
    entries = jnp.arange(count, dtype=jnp.int32)

    same = codes_here[:, None] == codes_here[None, :]
    earlier = entries[None, :] < entries[:, None]
    rank = jnp.sum((same & earlier).astype(jnp.int32), -1)

    slot = jnp.arange(2 * owners * CAP, dtype=jnp.int32).reshape(2 * owners, CAP, 1)
    chooser = (codes_here * CAP + rank == slot).astype(jnp.int32)
    source = jnp.sum(chooser * entries, -1).reshape(2, owners, CAP)

    about = jnp.concatenate([coef_index[0][:, None], offsets[0]], 1)
    notes = jnp.sum(chooser[..., None] * about, 2)
    notes = jnp.concatenate([notes, jnp.sum(chooser, -1)[..., None]], -1)
    notes = notes.reshape(2, owners, CAP, 4)

    forward, inverse, tap_lanes = transforms(extent)
    along_y, along_x = basis_filters()
    lanes_x = (along_x @ tap_lanes).astype(np.float32)
    basis = jnp.asarray(along_y.astype(np.float32))[:, :, None] * jnp.asarray(lanes_x)[:, None, :]
    tables = jnp.einsum(
        "ck,ksl->csl", coef_table, basis, precision=HIGHEST, preferred_element_type=jnp.float32
    )
    forward, inverse = jnp.asarray(forward), jnp.asarray(inverse)

    def swapped(value, partner):
        return lax.ppermute(value, "src", [(i, i ^ partner) for i in range(owners)])

    def towards(value, partner, axis=0):
        return lax.dynamic_index_in_dim(value, me ^ partner, axis, keepdims=False)

    told = {partner: swapped(towards(notes, partner, 1), partner) for partner in range(1, owners)}
    told[0] = towards(notes, 0, 1)

    def send(row_step, partner, after):
        picks = towards(source[row_step], partner)
        out = gather_tiles(tiles, variances, picks)
        if after is not None:
            out, after = lax.optimization_barrier((out, after))
        return swapped(out, partner), after

    def add(canvases, row_step, partner, held):
        if held is None:
            picks = towards(source[row_step], 0)
            held, spread, plane = tiles[None], variances[None], 0
        else:
            spread, plane = held, 1
            picks = jnp.arange(CAP, dtype=jnp.int32)
        note = told[partner][row_step]
        note = (note[:, 0], note[:, 1:3], note[:, 3])
        return place_tiles(
            canvases, held, spread, plane, picks, note, tables, forward, inverse
        )

    zero = jnp.zeros((patch, patch), jnp.float32)
    far = range(2, owners)
    arrived = {}
    for partner in far:
        arrived[1, partner], _ = send(1, partner, None)
    arrived[1, 1], _ = send(1, 1, None)
    arrived[0, 1], _ = send(0, 1, None)
    for partner in far:
        arrived[0, partner], arrived[1, partner] = send(0, partner, arrived[1, partner])

    ahead = (zero, zero)
    ahead = add(ahead, 1, 0, None)
    ahead = add(ahead, 1, 1, arrived[1, 1])
    here = add((zero, zero), 0, 0, None)
    here = add(here, 0, 1, arrived[0, 1])
    ahead, here = lax.optimization_barrier((ahead, here))
    for partner in far:
        ahead = add(ahead, 1, partner, arrived[1, partner])
    moved = [shifted(value, 1, 0) for value in ahead]
    for partner in far:
        here = add(here, 0, partner, arrived[0, partner])
    coadd = (here[0] + moved[0]) / (here[1] + moved[1] + 1.0)

    rim = detect_ra.shape[0] // 2
    along_dec = band(detect_dec, patch).T
    along_ra = band(detect_ra, patch)
    left = shifted(coadd[:, patch - rim :], 0, 1)
    right = shifted(coadd[:, :rim], 0, -1)

    def rows(first):
        return jnp.concatenate([part[first : first + rim] for part in (coadd, left, right)], 1)

    near = jnp.concatenate([shifted(rows(patch - rim), 1, 0), shifted(rows(0), -1, 0)], 0)
    middle, edges = inner_and_rims(along_dec, rim, 0)
    filtered = filter_columns(coadd, jnp.concatenate([left, right], 1), middle, edges)
    detection = filter_rows(
        filtered,
        near[:, :patch],
        near[:, patch:],
        middle,
        edges,
        *inner_and_rims(along_ra, rim, 1),
    )
    return (coadd, detection)


def solution(mesh):
    return jax.shard_map(
        on_device,
        mesh=mesh,
        in_specs=(
            P("sky", "src", None, None),
            P("sky", "src", None, None),
            P(),
            P("sky", "src"),
            P("sky", "src", None),
            P("sky", "src"),
            P(),
            P(),
        ),
        out_specs=(P("sky", "src"), P("sky", "src")),
        check_vma=False,
    )
```

```python
import functools

import ml_dtypes
import numpy as np
import jax
import jax.numpy as jnp
from jax import lax
from jax.experimental import pallas as pl
from jax.experimental.pallas import tpu as pltpu
from jax.sharding import PartitionSpec as P

CAP = 2
KSIZE = 21
SPREADS = (0.75, 1.5, 3.0)
LANES = 128
LEAD = 16
ROWS = 64
VMEM = 60 * 2**20
HIGHEST = lax.Precision.HIGHEST


def halves(value):
    high = value.astype(jnp.bfloat16)
    return high, (value - high.astype(jnp.float32)).astype(jnp.bfloat16)


def product_of(left, right):
    dot = functools.partial(jnp.dot, preferred_element_type=jnp.float32)
    return dot(left[1], right[0]) + dot(left[0], right[1]) + dot(left[0], right[0])


def basis_filters():
    centred = np.arange(KSIZE, dtype=np.float64) - KSIZE // 2
    along_x, along_y = [], []
    for spread in SPREADS:
        gaussian = np.exp(-(centred * centred) / (2.0 * spread * spread))
        scaled = centred / spread
        for power_x in range(5):
            for power_y in range(5 - power_x):
                filter_x = gaussian * scaled**power_x
                filter_y = gaussian * scaled**power_y
                along_x.append(filter_x / np.sum(np.abs(filter_x)))
                along_y.append(filter_y / np.sum(np.abs(filter_y)))
    return np.stack(along_y), np.stack(along_x)


def transforms(extent):
    radius = KSIZE // 2
    length = extent + 2 * radius
    main = extent // 2
    low = np.arange(main)
    high = np.arange(main, length // 2 + 1)
    extra = high.size
    step = 2.0 * np.pi / length

    def trig(points, freqs):
        angle = step * np.outer(points, freqs)
        return np.cos(angle), np.sin(angle)

    def packed(first, second):
        out = np.zeros((first.shape[0], LANES))
        out[:, :extra] = first
        out[:, extra : 2 * extra] = second
        return out

    pixels = np.arange(extent)
    taps = np.arange(KSIZE) - radius
    cos_low, sin_low = trig(pixels, low)
    cos_high, sin_high = trig(pixels, high)
    forward = np.concatenate(
        [cos_low, sin_low, packed(cos_high, sin_high), packed(sin_high, cos_high)], 1
    )
    gain_low = np.where(low == 0, 1.0, 2.0) / length
    gain_high = np.where(high == length // 2, 1.0, 2.0) / length
    inverse = np.concatenate(
        [cos_low * gain_low, sin_low * gain_low, packed(cos_high * gain_high, sin_high * gain_high)],
        1,
    ).T
    tap_cos_low, tap_sin_low = trig(taps, low)
    tap_cos_high, tap_sin_high = trig(taps, high)
    tap_lanes = np.concatenate(
        [
            tap_cos_low,
            tap_sin_low,
            packed(tap_cos_high, tap_cos_high),
            packed(tap_sin_high, -tap_sin_high),
        ],
        1,
    )
    def split(matrix):
        high = matrix.astype(ml_dtypes.bfloat16)
        return np.stack([high, (matrix - high.astype(np.float64)).astype(ml_dtypes.bfloat16)])

    return split(forward), split(inverse), tap_lanes


def place_kernel(
    patch,
    pick,
    coef,
    corner,
    fill,
    exp_ref,
    var_ref,
    table_ref,
    forward_ref,
    inverse_ref,
    numer_in,
    denom_in,
    numer_out,
    denom_out,
    spectrum,
    product,
    numer_acc,
    denom_acc,
):
    step = pl.program_id(0)
    extent = exp_ref.shape[-1]
    groups = spectrum.shape[0]
    half = (groups - 2) // 2
    radius = KSIZE // 2

    @pl.when(step == 0)
    def _():
        numer_acc[:patch, :] = numer_in[...]
        denom_acc[:patch, :] = denom_in[...]
        blank = jnp.zeros((8, patch), jnp.float32)
        numer_acc[patch:, :] = blank
        denom_acc[patch:, :] = blank
        edge = jnp.zeros((groups, LEAD, LANES), jnp.float32)
        spectrum[:, :LEAD, :] = edge
        spectrum[:, LEAD + extent :, :] = edge

    lines = product_of(halves(exp_ref[0, 0]), (forward_ref[0], forward_ref[1]))
    for group in range(groups):
        spectrum[group, LEAD : LEAD + extent, :] = lines[:, group * LANES : (group + 1) * LANES]

    def taps_of(tap, group):
        return table_ref[0, tap : tap + 1, group * LANES : (group + 1) * LANES]

    for base in range(0, extent, ROWS):
        for group in range(half):
            real = jnp.zeros((ROWS, LANES), jnp.float32)
            imag = jnp.zeros((ROWS, LANES), jnp.float32)
            for tap in range(KSIZE):
                at = base + tap + LEAD - radius
                cosine = spectrum[group, at : at + ROWS, :]
                sine = spectrum[half + group, at : at + ROWS, :]
                tap_cos = taps_of(tap, group)
                tap_sin = taps_of(tap, half + group)
                real = real + tap_cos * cosine + tap_sin * sine
                imag = imag + tap_cos * sine - tap_sin * cosine
            product[base : base + ROWS, group * LANES : (group + 1) * LANES] = real
            product[
                base : base + ROWS, (half + group) * LANES : (half + group + 1) * LANES
            ] = imag
        both = jnp.zeros((ROWS, LANES), jnp.float32)
        for tap in range(KSIZE):
            at = base + tap + LEAD - radius
            both = (
                both
                + taps_of(tap, groups - 2) * spectrum[groups - 2, at : at + ROWS, :]
                + taps_of(tap, groups - 1) * spectrum[groups - 1, at : at + ROWS, :]
            )
        product[base : base + ROWS, (groups - 2) * LANES :] = both

    matched = product_of(halves(product[...]), (inverse_ref[0], inverse_ref[1]))
    weight = fill[step].astype(jnp.float32) / var_ref[0, 0]
    row, col = corner[2 * step], corner[2 * step + 1]
    low_row = lax.rem(row, 8)
    first = pl.multiple_of(row - low_row, 8)

    def placed(tile):
        wide = jnp.concatenate([tile, jnp.zeros((extent, patch - extent), jnp.float32)], 1)
        wide = pltpu.roll(wide, col, 1)
        wide = jnp.concatenate([wide, jnp.zeros((8, patch), jnp.float32)], 0)
        return pltpu.roll(wide, low_row, 0)

    where = pl.ds(first, extent + 8)
    numer_acc[where, :] = numer_acc[where, :] + placed(weight * matched)
    denom_acc[where, :] = denom_acc[where, :] + placed(weight)

    @pl.when(step == pl.num_programs(0) - 1)
    def _():
        numer_out[...] = numer_acc[:patch, :]
        denom_out[...] = denom_acc[:patch, :]


def place_tiles(canvases, tiles, variance, plane, pick, about, tables, forward, inverse):
    coef, corner, fill = about
    patch = canvases[0].shape[0]
    extent = tiles.shape[-1]
    lanes = forward.shape[-1]
    count = pick.shape[0]

    def whole(*shape):
        return pl.BlockSpec(shape, lambda i, *refs: (0,) * len(shape))

    def tile_spec(which):
        return pl.BlockSpec(
            (1, 1, extent, extent), lambda i, pick, *refs: (which, pick[i], 0, 0)
        )

    grid_spec = pltpu.PrefetchScalarGridSpec(
        num_scalar_prefetch=4,
        grid=(count,),
        in_specs=[
            tile_spec(0),
            tile_spec(plane),
            pl.BlockSpec((1, KSIZE, lanes), lambda i, pick, coef, *refs: (coef[i], 0, 0)),
            whole(*forward.shape),
            whole(*inverse.shape),
            whole(patch, patch),
            whole(patch, patch),
        ],
        out_specs=[whole(patch, patch), whole(patch, patch)],
        scratch_shapes=[
            pltpu.VMEM((lanes // LANES, extent + 2 * LEAD, LANES), jnp.float32),
            pltpu.VMEM((extent, lanes - LANES), jnp.float32),
            pltpu.VMEM((patch + 8, patch), jnp.float32),
            pltpu.VMEM((patch + 8, patch), jnp.float32),
        ],
    )
    return pl.pallas_call(
        functools.partial(place_kernel, patch),
        grid_spec=grid_spec,
        out_shape=[jax.ShapeDtypeStruct((patch, patch), jnp.float32)] * 2,
        compiler_params=pltpu.CompilerParams(
            vmem_limit_bytes=VMEM
        ),
        cost_estimate=pl.CostEstimate(
            flops=count * 80 * extent * extent * lanes,
            bytes_accessed=16 * patch * patch + count * 8 * extent * extent,
            transcendentals=0,
        ),
    )(pick, coef, corner.reshape(-1), fill, tiles, variance, tables, forward, inverse, *canvases)


def gather_kernel(pick, exp_ref, var_ref, out_ref):
    out_ref[0] = exp_ref[...]
    out_ref[1] = var_ref[...]


def gather_tiles(tiles, variance, pick):
    extent = tiles.shape[-1]
    count = pick.shape[0]
    tile_spec = pl.BlockSpec((1, extent, extent), lambda i, pick: (pick[i], 0, 0))
    return pl.pallas_call(
        gather_kernel,
        grid_spec=pltpu.PrefetchScalarGridSpec(
            num_scalar_prefetch=1,
            grid=(count,),
            in_specs=[tile_spec, tile_spec],
            out_specs=pl.BlockSpec((2, 1, extent, extent), lambda i, pick: (0, i, 0, 0)),
        ),
        out_shape=jax.ShapeDtypeStruct((2, count, extent, extent), jnp.float32),
        compiler_params=pltpu.CompilerParams(vmem_limit_bytes=VMEM),
        cost_estimate=pl.CostEstimate(
            flops=0, bytes_accessed=16 * count * extent * extent, transcendentals=0
        ),
    )(pick, tiles, variance)


def band_kernel(taps_ref, out_ref):
    spread = jnp.broadcast_to(taps_ref[...], out_ref.shape)
    out_ref[...] = pltpu.roll(spread, 0, 1, stride=1, stride_axis=0)


def band(taps, outputs):
    size = taps.shape[0]
    width = outputs + LANES
    row = jnp.concatenate([taps, jnp.zeros((width - size,), jnp.float32)])[None]
    wide = pl.pallas_call(
        band_kernel,
        out_shape=jax.ShapeDtypeStruct((outputs, width), jnp.float32),
        in_specs=[pl.BlockSpec(memory_space=pltpu.VMEM)],
        out_specs=pl.BlockSpec(memory_space=pltpu.VMEM),
        compiler_params=pltpu.CompilerParams(vmem_limit_bytes=VMEM),
    )(row)
    return wide[:, : outputs + size - 1]


def inner_and_rims(matrix, rim, axis):
    size = matrix.shape[axis]
    cut = functools.partial(lax.slice_in_dim, matrix, axis=axis)
    return cut(rim, size - rim), jnp.concatenate([cut(0, rim), cut(size - rim, size)], axis)


def columns_kernel(rows_ref, edge_ref, middle_ref, edges_ref, out_ref):
    out_ref[...] = product_of(halves(rows_ref[...]), halves(middle_ref[...])) + product_of(
        halves(edge_ref[...]), halves(edges_ref[...])
    )


def rows_kernel(
    filtered_ref, near_ref, corner_ref, middle_ref, edges_ref, across_ref, rims_ref, out_ref
):
    outside = product_of(halves(near_ref[...]), halves(middle_ref[...])) + product_of(
        halves(corner_ref[...]), halves(edges_ref[...])
    )
    out_ref[...] = product_of(halves(across_ref[...]), halves(filtered_ref[...])) + product_of(
        halves(rims_ref[...]), halves(outside)
    )


def filter_call(kernel, *operands):
    return pl.pallas_call(
        kernel,
        out_shape=jax.ShapeDtypeStruct(operands[0].shape, jnp.float32),
        in_specs=[pl.BlockSpec(memory_space=pltpu.VMEM)] * len(operands),
        out_specs=pl.BlockSpec(memory_space=pltpu.VMEM),
        compiler_params=pltpu.CompilerParams(vmem_limit_bytes=VMEM),
        cost_estimate=pl.CostEstimate(
            flops=6 * operands[0].size * operands[0].shape[1],
            bytes_accessed=sum(4 * operand.size for operand in operands),
            transcendentals=0,
        ),
    )(*operands)


filter_columns = functools.partial(filter_call, columns_kernel)
filter_rows = functools.partial(filter_call, rows_kernel)


def shifted(value, sky_step, src_step):
    skies, owners = lax.axis_size("sky"), lax.axis_size("src")
    pairs = []
    for sky in range(skies):
        for src in range(owners):
            to = src + src_step
            if 0 <= to < owners:
                target = ((sky + sky_step) % skies) * owners + to
                pairs.append((sky * owners + src, target))
    return lax.ppermute(value, ("sky", "src"), pairs)


def on_device(
    exposures, variance, coef_table, coef_index, offsets, tile_codes, detect_ra, detect_dec
):
    owners = lax.axis_size("src")
    me = lax.axis_index("src")
    tiles, variances = exposures[0], variance[0]
    count, extent = tiles.shape[0], tiles.shape[-1]
    patch = 2 * extent
    codes_here = tile_codes[0]
    entries = jnp.arange(count, dtype=jnp.int32)

    same = codes_here[:, None] == codes_here[None, :]
    earlier = entries[None, :] < entries[:, None]
    rank = jnp.sum((same & earlier).astype(jnp.int32), -1)

    slot = jnp.arange(2 * owners * CAP, dtype=jnp.int32).reshape(2 * owners, CAP, 1)
    chooser = (codes_here * CAP + rank == slot).astype(jnp.int32)
    source = jnp.sum(chooser * entries, -1).reshape(2, owners, CAP)

    about = jnp.concatenate([coef_index[0][:, None], offsets[0]], 1)
    notes = jnp.sum(chooser[..., None] * about, 2)
    notes = jnp.concatenate([notes, jnp.sum(chooser, -1)[..., None]], -1)
    notes = notes.reshape(2, owners, CAP, 4)

    forward, inverse, tap_lanes = transforms(extent)
    along_y, along_x = basis_filters()
    lanes_x = (along_x @ tap_lanes).astype(np.float32)
    basis = jnp.asarray(along_y.astype(np.float32))[:, :, None] * jnp.asarray(lanes_x)[:, None, :]
    tables = jnp.einsum(
        "ck,ksl->csl", coef_table, basis, precision=HIGHEST, preferred_element_type=jnp.float32
    )
    forward, inverse = jnp.asarray(forward), jnp.asarray(inverse)

    def swapped(value, partner):
        return lax.ppermute(value, "src", [(i, i ^ partner) for i in range(owners)])

    def towards(value, partner, axis=0):
        return lax.dynamic_index_in_dim(value, me ^ partner, axis, keepdims=False)

    told = {partner: swapped(towards(notes, partner, 1), partner) for partner in range(1, owners)}
    told[0] = towards(notes, 0, 1)

    def send(row_step, partner, after):
        picks = towards(source[row_step], partner)
        out = gather_tiles(tiles, variances, picks)
        if after is not None:
            out, after = lax.optimization_barrier((out, after))
        return swapped(out, partner), after

    def add(canvases, row_step, partner, held):
        if held is None:
            picks = towards(source[row_step], 0)
            held, spread, plane = tiles[None], variances[None], 0
        else:
            spread, plane = held, 1
            picks = jnp.arange(CAP, dtype=jnp.int32)
        note = told[partner][row_step]
        note = (note[:, 0], note[:, 1:3], note[:, 3])
        return place_tiles(
            canvases, held, spread, plane, picks, note, tables, forward, inverse
        )

    zero = jnp.zeros((patch, patch), jnp.float32)
    far = range(2, owners)
    arrived = {}
    for partner in far:
        arrived[1, partner], _ = send(1, partner, None)
    arrived[1, 1], _ = send(1, 1, None)
    arrived[0, 1], _ = send(0, 1, None)
    for partner in far:
        arrived[0, partner], arrived[1, partner] = send(0, partner, arrived[1, partner])

    ahead = (zero, zero)
    ahead = add(ahead, 1, 0, None)
    ahead = add(ahead, 1, 1, arrived[1, 1])
    here = add((zero, zero), 0, 0, None)
    here = add(here, 0, 1, arrived[0, 1])
    for partner in far:
        ahead = add(ahead, 1, partner, arrived[1, partner])
    moved = [shifted(value, 1, 0) for value in ahead]
    for partner in far:
        here = add(here, 0, partner, arrived[0, partner])
    coadd = (here[0] + moved[0]) / (here[1] + moved[1] + 1.0)

    rim = detect_ra.shape[0] // 2
    along_dec = band(detect_dec, patch).T
    along_ra = band(detect_ra, patch)
    left = shifted(coadd[:, patch - rim :], 0, 1)
    right = shifted(coadd[:, :rim], 0, -1)

    def rows(first):
        return jnp.concatenate([part[first : first + rim] for part in (coadd, left, right)], 1)

    near = jnp.concatenate([shifted(rows(patch - rim), 1, 0), shifted(rows(0), -1, 0)], 0)
    middle, edges = inner_and_rims(along_dec, rim, 0)
    filtered = filter_columns(coadd, jnp.concatenate([left, right], 1), middle, edges)
    detection = filter_rows(
        filtered,
        near[:, :patch],
        near[:, patch:],
        middle,
        edges,
        *inner_and_rims(along_ra, rim, 1),
    )
    return (coadd, detection)


def solution(mesh):
    return jax.shard_map(
        on_device,
        mesh=mesh,
        in_specs=(
            P("sky", "src", None, None),
            P("sky", "src", None, None),
            P(),
            P("sky", "src"),
            P("sky", "src", None),
            P("sky", "src"),
            P(),
            P(),
        ),
        out_specs=(P("sky", "src"), P("sky", "src")),
        check_vma=False,
    )
```
